768 devices in a mesh: row: 48 (over z, x), rep: 16 (over y, core).
Axes of the slice: x: 4, y: 8, z: 12, core: 2. Of those that a mesh axis runs over, the one named last changes fastest.
Arguments:
- left_blocks: float32 [48, 128, 4096], P('row', 'rep'), may hold values from -0.75 to 0.75
- right_blocks: float32 [48, 16, 64, 4096], P('row', 'rep'), may hold values from -0.6 to 0.6
- task_right: int32 [48, 16, 1024], P('row', 'rep'), may hold values from 0 to 63
- task_slot: int32 [48, 16, 1024], P('row', 'rep'), may hold values from 0 to 95, as said below
- recv_owner: int32 [48, 96], P('row'), may hold values from 0 to 31, as said below
Outputs:
- owned_blocks: float32 [48, 32, 4096], P('row', 'rep')
The draws below stay inside these ranges and needn't reach their ends.
Inputs may be any that keep to these rules, and one draw needn't show every extreme that they name: `task_slot`: each device's list names every one of its 96 slots. `recv_owner`: each row index's list names every one of its 32 blocks.
All inputs are finite; a program needn't handle non-finite values.
Results may differ from the reference program's by a relative error of at most 0.0003.
Values sent between devices are 32-bit elements; how exact they have to be, the bound alone decides.
No kernel may reach another device: no remote copies, remote signals or barrier semaphores. Data moves between devices by JAX's collectives and lax.ppermute only.
A program may use at most 32 MiB of HBM per device.

```python
import jax
import jax.numpy as jnp
from jax import lax

BS = 64
BLK = 4096
LB = 8
RB = 64
TASK_DEV = 1024
CAP = 2
PRODUCT_SLOTS = 96
OWNED_PRODUCTS = 32
N_ROW = 48
N_REP = 16


def draw_task_slot(key, part):
    key = jax.random.fold_in(key, 11)
    leading_key, trailing_key, third_key = jax.random.split(key, 3)
    array_extent = (N_ROW, N_REP, TASK_DEV)
    leading_selection = jax.random.randint(leading_key, array_extent, 0, PRODUCT_SLOTS)
    trailing_selection = jax.random.randint(trailing_key, array_extent, 0, PRODUCT_SLOTS)
    shifted_rows = jnp.minimum(leading_selection, trailing_selection)
    child_keys = jax.random.split(third_key, N_ROW * N_REP)
    device_ranks = jax.vmap(lambda child_key: jax.random.permutation(child_key, TASK_DEV))(child_keys)
    device_ranks = device_ranks.reshape(array_extent).astype(jnp.int32)
    return jnp.where(device_ranks < PRODUCT_SLOTS, device_ranks, shifted_rows).astype(jnp.int32)


def draw_recv_owner(key, part):
    key = jax.random.fold_in(key, 23)
    leading_key, trailing_key = jax.random.split(key, 2)
    padding_value = jax.random.randint(leading_key, (N_ROW, PRODUCT_SLOTS), 0, OWNED_PRODUCTS)
    child_keys = jax.random.split(trailing_key, N_ROW)
    device_ranks = jax.vmap(lambda child_key: jax.random.permutation(child_key, PRODUCT_SLOTS))(child_keys).astype(jnp.int32)
    return jnp.where(device_ranks < OWNED_PRODUCTS, device_ranks, padding_value).astype(jnp.int32)


def plant(entries, rng, least, largest):
    spot = [jax.random.randint(jax.random.fold_in(rng, axis), (), 0, length) for axis, length in enumerate(entries.shape)]
    widest = entries.shape.index(max(entries.shape))
    neighbour = spot[:widest] + [(spot[widest] + 1) % entries.shape[widest]] + spot[widest + 1:]
    return entries.at[tuple(spot)].set(least).at[tuple(neighbour)].set(largest)


def block_levels(stream_key, dims, shards, low, top_value):
    loudness, own = 1.0, jax.random.fold_in(stream_key, 6)
    for position, blocks in shards:
        heights = jnp.exp(jax.random.uniform(jax.random.fold_in(own, position), (blocks,), jnp.float32, low / len(shards), top_value / len(shards)))
        loudness = loudness * jnp.repeat(heights, dims[position] // blocks).reshape([-1 if axis == position else 1 for axis in range(len(dims))])
    return loudness


def normal_values(key, shape, deviation, bound, shards=(), kind=jnp.bfloat16):
    drawn = jax.random.normal(key, shape, jnp.float32) * deviation
    if len(shards) > 0:
        drawn = block_levels(key, shape, shards, -0.22, 0.18) * drawn
    return jnp.clip(drawn, min=-bound, max=bound).astype(kind)


def setup_inputs(seed: int = 0) -> dict:
    key_list = jax.random.split(jax.random.key(seed), 6)
    left_blocks = normal_values(key_list[0], (N_ROW, N_REP * LB, BLK), BS ** -0.5, 0.75, ((0, 48), (1, 16)), jnp.float32)
    right_blocks = normal_values(key_list[1], (N_ROW, N_REP, RB, BLK), 0.1, 0.6, ((0, 48), (1, 16)), jnp.float32)
    task_right = plant(jax.random.randint(key_list[2], (N_ROW, N_REP, TASK_DEV), 0, RB), jax.random.fold_in(key_list[2], 1), 0, RB - 1).astype(jnp.int32)
    task_slot = draw_task_slot(jax.random.fold_in(key_list[5], 71), 0)
    recv_owner = draw_recv_owner(jax.random.fold_in(key_list[5], 71), 0)
    return dict(left_blocks=left_blocks, right_blocks=right_blocks, task_right=task_right, task_slot=task_slot, recv_owner=recv_owner)


def reference(left_blocks, right_blocks, task_right, task_slot, recv_owner):
    per_block = TASK_DEV // (N_REP * LB)
    slot_count = N_ROW * CAP

    def one_device(left_panel, rights, picks, targets):
        left_group = left_panel.reshape(N_REP * LB, BS, BS)
        right_rows = rights[picks].reshape(N_REP * LB, per_block, BS, BS)
        products = jnp.einsum("kij,ktjl->ktil", left_group, right_rows, precision=lax.Precision.HIGHEST)
        products = products.reshape(TASK_DEV, BS * BS)
        return jax.ops.segment_sum(products, targets, num_segments=slot_count)

    def per_row(source):
        def over_rep(running, member):
            return running + one_device(left_blocks[source], right_blocks[source, member], task_right[source, member], task_slot[source, member]), None
        start_value = jnp.zeros((slot_count, BS * BS), jnp.float32)
        summed, unused = lax.scan(over_rep, start_value, jnp.arange(N_REP, dtype=jnp.int32))
        return summed

    totals = lax.map(per_row, jnp.arange(N_ROW, dtype=jnp.int32))

    def per_owner(target):
        block_rows = lax.dynamic_slice_in_dim(totals, (target * CAP).astype(jnp.int32), CAP, 1)
        received = block_rows.reshape(slot_count, BS * BS)
        return jax.ops.segment_sum(received, recv_owner[target], num_segments=OWNED_PRODUCTS)

    return lax.map(per_owner, jnp.arange(N_ROW, dtype=jnp.int32))
```

```python
import jax
import jax.numpy as jnp
from jax import lax
from jax.experimental import pallas as pl
from jax.experimental.pallas import tpu as pltpu
from jax.sharding import Mesh
from jax.sharding import PartitionSpec as P

BS = 64
BLK = BS * BS
OWN_DEV = 2
ROWS = BLK // 128


def low_half(shape):
    return lax.broadcasted_iota(jnp.int32, shape, len(shape) - 1) < BS


def split_rights(right_ref, low_ref, high_ref, spread_ref):
    count = right_ref.shape[0]
    mask8 = low_half((8, 128))

    def unfold(group, carry):
        base = pl.multiple_of(group * 8, 8)
        for m in range(ROWS):
            x = right_ref[pl.ds(base, 8), m * 128 : (m + 1) * 128]
            turned = pltpu.roll(x, BS, 1)
            spread_ref[pl.ds(base * BS + 2 * m, 8, stride=BS), :] = jnp.where(mask8, x, turned)
            spread_ref[pl.ds(base * BS + 2 * m + 1, 8, stride=BS), :] = jnp.where(mask8, turned, x)
        return carry

    lax.fori_loop(0, count // 8, unfold, 0)
    mask = low_half((BS, 128))

    def cut(block, carry):
        x = spread_ref[pl.ds(pl.multiple_of(block * BS, BS), BS), :]
        coarse = x.astype(jnp.bfloat16).astype(jnp.float32)
        fine = x - coarse
        both = jnp.concatenate([coarse, fine], axis=0)
        m2 = jnp.concatenate([mask, mask], axis=0)
        low_ref[block] = jnp.where(m2, both, 0.0).astype(jnp.bfloat16)
        high_ref[block] = jnp.where(m2, 0.0, both).astype(jnp.bfloat16)
        return carry

    lax.fori_loop(0, count, cut, 0, unroll=2)


def prepare(rights):
    count = rights.shape[0]
    half = jax.ShapeDtypeStruct((count, 2 * BS, 128), jnp.bfloat16)
    return pl.pallas_call(
        split_rights,
        out_shape=(half, half),
        scratch_shapes=[pltpu.VMEM((count * BS, 128), jnp.float32)],
        compiler_params=pltpu.CompilerParams(vmem_limit_bytes=32 * 1024 * 1024),
        cost_estimate=pl.CostEstimate(flops=8 * count * BLK, bytes_accessed=12 * count * BLK, transcendentals=0),
        name="split_rights",
    )(rights)


def multiply(
    core_ref, pick_ref, slot_ref, left_ref, low_ref, high_ref, mine_ref, other_ref, flat_ref, acc0, acc1, acc2, acc3, nat_ref
):
    count = left_ref.shape[0]
    per_block = pick_ref.shape[0] // count
    slot_count = acc0.shape[0]
    accs = (acc0, acc1, acc2, acc3)

    def clear(s, carry):
        for acc in accs:
            acc[s] = jnp.zeros(acc.shape[1:], jnp.float32)
        return carry

    lax.fori_loop(0, slot_count, clear, 0)

    def unfold(group, carry):
        base = pl.multiple_of(group * 8, 8)
        for m in range(ROWS):
            flat_ref[pl.ds(base * ROWS + m, 8, stride=ROWS), :] = left_ref[pl.ds(base, 8), m * 128 : (m + 1) * 128]
        return carry

    lax.fori_loop(0, count // 8, unfold, 0)
    mask = low_half((ROWS, 128))

    def one_block(k, carry):
        x = flat_ref[pl.ds(pl.multiple_of(k * ROWS, ROWS), ROWS), :]
        coarse = x.astype(jnp.bfloat16).astype(jnp.float32)
        fine = x - coarse
        even = jnp.where(mask, coarse, pltpu.roll(fine, BS, 1))
        odd = jnp.where(mask, pltpu.roll(coarse, BS, 1), fine)
        tall = jnp.concatenate([even, odd], axis=0).astype(jnp.bfloat16)
        lhs = jnp.concatenate([tall, tall], axis=1)
        first = k * per_block
        for quad in range(per_block // 4):
            pairs = []
            for pair in range(2):
                t = first + quad * 4 + pair * 2
                pairs.append(low_ref[pick_ref[t]] + high_ref[pick_ref[t + 1]])
            both = jnp.concatenate(pairs, axis=1)
            rhs = jnp.concatenate([both[:BS], both[:BS], both[BS:], both[BS:]], axis=0)
            out = jnp.dot(lhs, rhs, preferred_element_type=jnp.float32)
            for pair in range(2):
                t = first + quad * 4 + pair * 2
                part = out[:, pair * 128 : (pair + 1) * 128]
                accs[2 * pair][slot_ref[t]] += part
                accs[2 * pair + 1][slot_ref[t + 1]] += part
        return carry

    lax.fori_loop(0, count, one_block, 0, unroll=8)

    def fold(s, carry):
        low = acc0[s] + acc2[s]
        high = acc1[s] + acc3[s]
        even = low[:ROWS] + pltpu.roll(high[:ROWS], BS, 1)
        odd = pltpu.roll(low[ROWS:], BS, 1) + high[ROWS:]
        nat_ref[pl.ds(pl.multiple_of(s * ROWS, ROWS), ROWS), :] = jnp.where(mask, even, odd)
        return carry

    lax.fori_loop(0, slot_count, fold, 0, unroll=8)

    pieces = mine_ref.shape[0]
    tiles = ROWS // (2 * pieces)
    core = core_ref[0]

    def place(group, carry):
        base = pl.multiple_of(group * 8, 8)
        for out_ref, half in ((mine_ref, core), (other_ref, 1 - core)):
            first = base * ROWS + half * (ROWS // 2)
            for m in range(ROWS // 2):
                out_ref[m // tiles, pl.ds(base, 8), (m % tiles) * 128 : (m % tiles + 1) * 128] = nat_ref[
                    pl.ds(first + m, 8, stride=ROWS), :
                ]
        return carry

    lax.fori_loop(0, slot_count // 8, place, 0)


def products(core, picks, targets, panel, low, high, slot_count, pieces):
    smem = pl.BlockSpec(memory_space=pltpu.SMEM)
    vmem = pl.BlockSpec(memory_space=pltpu.VMEM)
    acc = pltpu.VMEM((slot_count, BS, 128), jnp.float32)
    out = jax.ShapeDtypeStruct((pieces, slot_count, BLK // (2 * pieces)), jnp.float32)
    flops = 2 * picks.shape[0] * BS * BS * BS * 4
    return pl.pallas_call(
        multiply,
        out_shape=(out, out),
        in_specs=[smem, smem, smem, vmem, vmem, vmem],
        out_specs=(vmem, vmem),
        scratch_shapes=[
            pltpu.VMEM((panel.shape[0] * ROWS, 128), jnp.float32),
            acc,
            acc,
            acc,
            acc,
            pltpu.VMEM((slot_count * ROWS, 128), jnp.float32),
        ],
        compiler_params=pltpu.CompilerParams(vmem_limit_bytes=48 * 1024 * 1024),
        cost_estimate=pl.CostEstimate(flops=flops, bytes_accessed=8 * 1024 * 1024, transcendentals=0),
        name="multiply",
    )(core, picks, targets, panel, low, high)


def local(left_blocks, right_blocks, task_right, task_slot, recv_owner):
    row_count = lax.axis_size("row")
    chips = lax.axis_size("y")
    group = ("y", "core")
    members = 2 * chips
    slot_count = recv_owner.shape[1]
    capacity = slot_count // row_count
    core = lax.axis_index("core").astype(jnp.int32).reshape(1)

    panel = lax.all_gather(left_blocks[0], group, axis=0, tiled=True)
    low, high = prepare(right_blocks[0, 0])
    mine, other = products(core, task_right[0, 0], task_slot[0, 0], panel, low, high, slot_count, chips)
    mine = mine + lax.ppermute(other, "core", [(0, 1), (1, 0)])
    pieces = lax.all_to_all(mine, "y", split_axis=0, concat_axis=0, tiled=True)
    width = pieces.shape[2]
    piece = pieces.sum(axis=0).reshape(row_count, capacity, width)
    received = lax.all_to_all(piece, "row", split_axis=0, concat_axis=0, tiled=True).reshape(slot_count, width)
    owners = recv_owner[0]
    owned_ids = jnp.arange(OWN_DEV * members, dtype=jnp.int32)
    selector = (owners[None, :] == owned_ids[:, None]).astype(jnp.float32)
    owned = jnp.dot(selector, received, precision=lax.Precision.HIGHEST, preferred_element_type=jnp.float32)
    own = lax.all_to_all(
        owned.reshape(members, OWN_DEV, width), group, split_axis=0, concat_axis=0, tiled=True
    )
    own = own.reshape(chips, 2, OWN_DEV, width).transpose(2, 1, 0, 3)
    return own.reshape(1, OWN_DEV, BLK)


def solution(mesh):
    fine = Mesh(mesh.devices.reshape(mesh.shape["row"], mesh.shape["rep"] // 2, 2), ("row", "y", "core"))
    group = ("y", "core")
    in_specs = (
        P("row", group, None),
        P("row", group, None, None),
        P("row", group, None),
        P("row", group, None),
        P("row", None),
    )
    out_specs = P("row", group, None)
    return jax.shard_map(local, mesh=fine, in_specs=in_specs, out_specs=out_specs, check_vma=False)
```

```python
import jax
import jax.numpy as jnp
from jax import lax
from jax.experimental import pallas as pl
from jax.experimental.pallas import tpu as pltpu
from jax.sharding import Mesh
from jax.sharding import PartitionSpec as P

BS = 64
BLK = BS * BS
OWN_DEV = 2
ROWS = BLK // 128
SWAP = [(0, 1), (1, 0)]


def low_half(shape):
    return lax.broadcasted_iota(jnp.int32, shape, len(shape) - 1) < BS


def split_rights(right_ref, parts_ref, spread_ref):
    count = right_ref.shape[0]
    mask = low_half((8, 128))

    def unfold(group, carry):
        base = pl.multiple_of(group * 8, 8)
        for m in range(ROWS):
            x = right_ref[pl.ds(base, 8), m * 128 : (m + 1) * 128]
            turned = pltpu.roll(x, BS, 1)
            spread_ref[pl.ds(base * BS + 2 * m, 8, stride=BS), :] = jnp.where(mask, x, turned)
            spread_ref[pl.ds(base * BS + 2 * m + 1, 8, stride=BS), :] = jnp.where(mask, turned, x)
        return carry

    lax.fori_loop(0, count // 8, unfold, 0)

    def cut(block, carry):
        x = spread_ref[pl.ds(pl.multiple_of(block * BS, BS), BS), :]
        coarse = x.astype(jnp.bfloat16)
        parts_ref[block, :BS, :] = coarse
        parts_ref[block, BS:, :] = (x - coarse.astype(jnp.float32)).astype(jnp.bfloat16)
        return carry

    lax.fori_loop(0, count, cut, 0, unroll=4)


def prepare(rights):
    count = rights.shape[0]
    return pl.pallas_call(
        split_rights,
        out_shape=jax.ShapeDtypeStruct((count, 2 * BS, 128), jnp.bfloat16),
        scratch_shapes=[pltpu.VMEM((count * BS, 128), jnp.float32)],
        compiler_params=pltpu.CompilerParams(vmem_limit_bytes=16 * 1024 * 1024),
        cost_estimate=pl.CostEstimate(flops=8 * count * BLK, bytes_accessed=12 * count * BLK, transcendentals=0),
        name="split_rights",
    )(rights)


def multiply(
    core_ref, own_tasks_ref, twin_tasks_ref, left_ref, own_ref, twin_ref, mine_ref, other_ref,
    flat_ref, acc0, acc1, acc2, acc3, nat_ref,
):
    chips, share = left_ref.shape[0], left_ref.shape[1]
    count = chips * share
    per_block = own_tasks_ref.shape[1] // (2 * count)
    slot_count = acc0.shape[0]
    accs = (acc0, acc1, acc2, acc3)
    core = core_ref[0]

    def clear(s, carry):
        for acc in accs:
            acc[s] = jnp.zeros(acc.shape[1:], jnp.float32)
        return carry

    lax.fori_loop(0, slot_count, clear, 0, unroll=4)

    def unfold(chip, carry):
        for m in range(ROWS):
            flat_ref[pl.ds(chip * share * ROWS + m, share, stride=ROWS), :] = left_ref[chip, :, m * 128 : (m + 1) * 128]
        return carry

    lax.fori_loop(0, chips, unfold, 0)
    mask = low_half((ROWS, 128))
    wide = low_half((2 * BS, 128))

    def one_block(k, carry):
        x = flat_ref[pl.ds(pl.multiple_of(k * ROWS, ROWS), ROWS), :]
        coarse = x.astype(jnp.bfloat16).astype(jnp.float32)
        fine = x - coarse
        even = jnp.where(mask, coarse, pltpu.roll(fine, BS, 1))
        odd = jnp.where(mask, pltpu.roll(coarse, BS, 1), fine)
        tall = jnp.concatenate([even, odd], axis=0).astype(jnp.bfloat16)
        lhs = jnp.concatenate([tall, tall], axis=1)
        first = ((k // share) * 2 * share + core * share + k % share) * per_block
        for tasks_ref, parts_ref in ((own_tasks_ref, own_ref), (twin_tasks_ref, twin_ref)):
            for quad in range(per_block // 4):
                pairs = []
                for pair in range(2):
                    t = first + quad * 4 + pair * 2
                    pairs.append(jnp.where(wide, parts_ref[tasks_ref[0, t]], parts_ref[tasks_ref[0, t + 1]]))
                both = jnp.concatenate(pairs, axis=1)
                rhs = jnp.concatenate([both[:BS], both[:BS], both[BS:], both[BS:]], axis=0)
                out = jnp.dot(lhs, rhs, preferred_element_type=jnp.float32)
                for pair in range(2):
                    t = first + quad * 4 + pair * 2
                    part = out[:, pair * 128 : (pair + 1) * 128]
                    accs[2 * pair][tasks_ref[1, t]] += part
                    accs[2 * pair + 1][tasks_ref[1, t + 1]] += part
        return carry

    lax.fori_loop(0, count, one_block, 0, unroll=8)

    def fold(s, carry):
        low = acc0[s] + acc2[s]
        high = acc1[s] + acc3[s]
        even = low[:ROWS] + pltpu.roll(high[:ROWS], BS, 1)
        odd = pltpu.roll(low[ROWS:], BS, 1) + high[ROWS:]
        nat_ref[pl.ds(pl.multiple_of(s * ROWS, ROWS), ROWS), :] = jnp.where(mask, even, odd)
        return carry

    lax.fori_loop(0, slot_count, fold, 0, unroll=8)

    tiles = ROWS // (2 * mine_ref.shape[0])

    def place(group, carry):
        base = pl.multiple_of(group * 8, 8)
        for out_ref, half in ((mine_ref, core), (other_ref, 1 - core)):
            first = base * ROWS + half * (ROWS // 2)
            for m in range(ROWS // 2):
                out_ref[m // tiles, pl.ds(base, 8), (m % tiles) * 128 : (m % tiles + 1) * 128] = nat_ref[
                    pl.ds(first + m, 8, stride=ROWS), :
                ]
        return carry

    lax.fori_loop(0, slot_count // 8, place, 0)


def products(core, own_tasks, twin_tasks, panel, own, twin, slot_count):
    chips, share, _ = panel.shape
    smem = pl.BlockSpec(memory_space=pltpu.SMEM)
    vmem = pl.BlockSpec(memory_space=pltpu.VMEM)
    acc = pltpu.VMEM((slot_count, BS, 128), jnp.float32)
    out = jax.ShapeDtypeStruct((chips, slot_count, BLK // (2 * chips)), jnp.float32)
    flops = 2 * own_tasks.shape[1] * BS * BS * BS * 4
    return pl.pallas_call(
        multiply,
        out_shape=(out, out),
        in_specs=[smem, smem, smem, vmem, vmem, vmem],
        out_specs=(vmem, vmem),
        scratch_shapes=[
            pltpu.VMEM((chips * share * ROWS, 128), jnp.float32),
            acc,
            acc,
            acc,
            acc,
            pltpu.VMEM((slot_count * ROWS, 128), jnp.float32),
        ],
        compiler_params=pltpu.CompilerParams(vmem_limit_bytes=32 * 1024 * 1024),
        cost_estimate=pl.CostEstimate(flops=flops, bytes_accessed=8 * 1024 * 1024, transcendentals=0),
        name="multiply",
    )(core, own_tasks, twin_tasks, panel, own, twin)


def exchange(x, axis):
    return lax.all_to_all(x, axis, split_axis=0, concat_axis=0, tiled=True)


def local(left_blocks, right_blocks, task_right, task_slot, recv_owner):
    row_count = lax.axis_size("row")
    chips = lax.axis_size("y")
    group = ("y", "core")
    members = 2 * chips
    slot_count = recv_owner.shape[1]
    capacity = slot_count // row_count
    core = lax.axis_index("core").astype(jnp.int32).reshape(1)

    panel = exchange(jnp.broadcast_to(left_blocks, (chips,) + left_blocks.shape[1:]), "y")
    rights = right_blocks[0, 0]
    tasks = jnp.concatenate([task_right[0], task_slot[0]], axis=0)
    twin_rights = lax.ppermute(rights, "core", SWAP)
    twin_tasks = lax.ppermute(tasks, "core", SWAP)
    own = prepare(rights)
    twin = prepare(twin_rights)
    mine, other = products(core, tasks, twin_tasks, panel, own, twin, slot_count)
    mine = mine + lax.ppermute(other, "core", SWAP)
    pieces = exchange(mine, "y")
    width = pieces.shape[2]
    piece = pieces.sum(axis=0).reshape(row_count, capacity, width)
    received = exchange(piece, "row").reshape(slot_count, width)
    owners = recv_owner[0]
    owned_ids = jnp.arange(OWN_DEV * members, dtype=jnp.int32)
    selector = (owners[None, :] == owned_ids[:, None]).astype(jnp.float32)
    owned = jnp.dot(selector, received, precision=lax.Precision.HIGHEST, preferred_element_type=jnp.float32)
    own_blocks = exchange(owned.reshape(members, OWN_DEV, width), group)
    own_blocks = own_blocks.reshape(chips, 2, OWN_DEV, width).transpose(2, 1, 0, 3)
    return own_blocks.reshape(1, OWN_DEV, BLK)


def solution(mesh):
    fine = Mesh(mesh.devices.reshape(mesh.shape["row"], mesh.shape["rep"] // 2, 2), ("row", "y", "core"))
    group = ("y", "core")
    in_specs = (
        P("row", group, None),
        P("row", group, None, None),
        P("row", group, None),
        P("row", group, None),
        P("row", None),
    )
    out_specs = P("row", group, None)
    return jax.shard_map(local, mesh=fine, in_specs=in_specs, out_specs=out_specs, check_vma=False)
```

```python
import jax
import jax.numpy as jnp
from jax import lax
from jax.experimental import pallas as pl
from jax.experimental.pallas import tpu as pltpu
from jax.sharding import Mesh
from jax.sharding import PartitionSpec as P

BS = 64
BLK = BS * BS
OWN_DEV = 2
CAPACITY = 2
COLUMNS = 4
VMEM_LIMIT = 24 * 1024 * 1024
ROWS = BLK // 128
FLAT = ROWS + 8
SWAP = [(0, 1), (1, 0)]


def low_half(shape):
    return lax.broadcasted_iota(jnp.int32, shape, len(shape) - 1) < BS


def split_rights(own_ref, twin_ref, parts_ref, spread_ref):
    count = own_ref.shape[0]
    mask = low_half((8, 128))

    for side, right_ref in enumerate((own_ref, twin_ref)):

        def unfold(group, carry, right_ref=right_ref, side=side):
            base = pl.multiple_of(group * 8, 8)
            spot = (side * count + base) * BS
            for m in range(ROWS):
                x = right_ref[pl.ds(base, 8), m * 128 : (m + 1) * 128]
                turned = pltpu.roll(x, BS, 1)
                spread_ref[pl.ds(spot + 2 * m, 8, stride=BS), :] = jnp.where(mask, x, turned)
                spread_ref[pl.ds(spot + 2 * m + 1, 8, stride=BS), :] = jnp.where(mask, turned, x)
            return carry

        lax.fori_loop(0, count // 8, unfold, 0)

    def cut(block, carry):
        x = spread_ref[pl.ds(pl.multiple_of(block * BS, BS), BS), :]
        coarse = x.astype(jnp.bfloat16)
        parts_ref[block, :BS, :] = coarse
        parts_ref[block, BS:, :] = (x - coarse.astype(jnp.float32)).astype(jnp.bfloat16)
        return carry

    lax.fori_loop(0, 2 * count, cut, 0, unroll=4)


def prepare(own, twin):
    count = own.shape[0]
    return pl.pallas_call(
        split_rights,
        out_shape=jax.ShapeDtypeStruct((2 * count, 2 * BS, 128), jnp.bfloat16),
        in_specs=[pl.BlockSpec(memory_space=pltpu.VMEM)] * 2,
        out_specs=pl.BlockSpec(memory_space=pltpu.VMEM),
        scratch_shapes=[pltpu.VMEM((2 * count * BS, 128), jnp.float32)],
        compiler_params=pltpu.CompilerParams(vmem_limit_bytes=VMEM_LIMIT),
        cost_estimate=pl.CostEstimate(flops=16 * count * BLK, bytes_accessed=24 * count * BLK, transcendentals=0),
        name="split_rights",
    )(own, twin)


def copy_out(x_ref, out_hbm, sems):
    copies = [pltpu.make_async_copy(x_ref, out_hbm.at[i], sems.at[i]) for i in range(out_hbm.shape[0])]
    for copy in copies:
        copy.start()
    for copy in copies:
        copy.wait()


def repeat(x, count):
    return pl.pallas_call(
        copy_out,
        out_shape=jax.ShapeDtypeStruct((count,) + x.shape, x.dtype),
        in_specs=[pl.BlockSpec(memory_space=pltpu.VMEM)],
        out_specs=pl.BlockSpec(memory_space=pltpu.HBM),
        scratch_shapes=[pltpu.SemaphoreType.DMA((count,))],
        name="repeat",
    )(x)


def multiply(
    core_ref, own_tasks_hbm, twin_tasks_hbm, left_ref, parts_hbm, mine_ref, other_ref,
    own_tasks_ref, twin_tasks_ref, parts_ref, flat_ref, lhs_ref, acc0, acc1, nat_ref, sems,
):
    copies = [
        pltpu.make_async_copy(source, target, sems.at[i])
        for i, (source, target) in enumerate(
            ((own_tasks_hbm, own_tasks_ref), (twin_tasks_hbm, twin_tasks_ref), (parts_hbm, parts_ref))
        )
    ]
    for copy in copies:
        copy.start()
    chips, share = left_ref.shape[0], left_ref.shape[1]
    count = chips * share
    per_block = own_tasks_ref.shape[1] // (2 * count)
    slot_count = acc0.shape[0]
    rights = parts_ref.shape[0] // 2
    core = core_ref[0]

    def clear(s, carry):
        acc0[s] = jnp.zeros(acc0.shape[1:], jnp.float32)
        acc1[s] = jnp.zeros(acc1.shape[1:], jnp.float32)
        return carry

    lax.fori_loop(0, slot_count, clear, 0, unroll=8)

    def unfold(chip, carry):
        for m in range(ROWS):
            flat_ref[pl.ds(chip * share * FLAT + m, share, stride=FLAT), :] = left_ref[chip, :, m * 128 : (m + 1) * 128]
        return carry

    lax.fori_loop(0, chips, unfold, 0)
    mask = low_half((ROWS, 128))
    wide = low_half((2 * BS, 128))

    def cut(k, carry):
        x = flat_ref[pl.ds(pl.multiple_of(k * FLAT, 8), ROWS), :]
        coarse = x.astype(jnp.bfloat16).astype(jnp.float32)
        fine = x - coarse
        lhs_ref[k, :ROWS, :] = jnp.where(mask, coarse, pltpu.roll(fine, BS, 1)).astype(jnp.bfloat16)
        lhs_ref[k, ROWS:, :] = jnp.where(mask, pltpu.roll(coarse, BS, 1), fine).astype(jnp.bfloat16)
        return carry

    lax.fori_loop(0, count, cut, 0, unroll=8)
    for copy in copies:
        copy.wait()

    def one_block(k, carry):
        tall = lhs_ref[k]
        lhs = jnp.concatenate([tall, tall], axis=1)
        first = ((k // share) * 2 * share + core * share + k % share) * per_block
        for side, tasks_ref in enumerate((own_tasks_ref, twin_tasks_ref)):
            for quad in range(per_block // 4):
                pairs = []
                for pair in range(2):
                    t = first + quad * 4 + pair * 2
                    low = parts_ref[side * rights + tasks_ref[0, t]]
                    high = parts_ref[side * rights + tasks_ref[0, t + 1]]
                    pairs.append(jnp.where(wide, low, high))
                both = jnp.concatenate(pairs, axis=1)
                rhs = jnp.concatenate([both[:BS], both[:BS], both[BS:], both[BS:]], axis=0)
                out = jnp.dot(lhs, rhs, preferred_element_type=jnp.float32)
                for pair in range(2):
                    t = first + quad * 4 + pair * 2
                    part = out[:, pair * 128 : (pair + 1) * 128]
                    acc0[tasks_ref[1, t]] += part
                    acc1[tasks_ref[1, t + 1]] += part
        return carry

    lax.fori_loop(0, count, one_block, 0, unroll=16)

    columns, _, run = mine_ref.shape[:3]
    capacity = CAPACITY

    def fold(s, carry):
        owner = s // capacity
        spot = (owner % columns) * run + (owner // columns) * capacity + s % capacity
        low, high = acc0[s], acc1[s]
        even = low[:ROWS] + pltpu.roll(high[:ROWS], BS, 1)
        odd = pltpu.roll(low[ROWS:], BS, 1) + high[ROWS:]
        nat_ref[pl.ds(pl.multiple_of(spot * FLAT, 8), ROWS), :] = jnp.where(mask, even, odd)
        return carry

    lax.fori_loop(0, slot_count, fold, 0, unroll=16)

    tiles = ROWS // (2 * chips)

    def place(column, carry):
        for group in range(run // 8):
            for out_ref, half in ((mine_ref, core), (other_ref, 1 - core)):
                first = (column * run + group * 8) * FLAT + half * (ROWS // 2)
                for m in range(ROWS // 2):
                    out_ref[column, m // tiles, group * 8 : (group + 1) * 8, (m % tiles) * 128 : (m % tiles + 1) * 128] = (
                        nat_ref[pl.ds(first + m, 8, stride=FLAT), :]
                    )
        return carry

    lax.fori_loop(0, columns, place, 0)


def products(core, own_tasks, twin_tasks, panel, parts, slot_count, columns):
    chips, share, _ = panel.shape
    smem = pl.BlockSpec(memory_space=pltpu.SMEM)
    vmem = pl.BlockSpec(memory_space=pltpu.VMEM)
    anywhere = pl.BlockSpec(memory_space=pl.ANY)
    acc = pltpu.VMEM((slot_count, BS, 128), jnp.float32)
    out = jax.ShapeDtypeStruct((columns, chips, slot_count // columns, BLK // (2 * chips)), jnp.float32)
    flops = 2 * own_tasks.shape[1] * BS * BS * BS * 4
    return pl.pallas_call(
        multiply,
        out_shape=(out, out),
        in_specs=[smem, anywhere, anywhere, vmem, pl.BlockSpec(memory_space=pltpu.HBM)],
        out_specs=(vmem, vmem),
        scratch_shapes=[
            pltpu.SMEM(own_tasks.shape, jnp.int32),
            pltpu.SMEM(twin_tasks.shape, jnp.int32),
            pltpu.VMEM(parts.shape, parts.dtype),
            pltpu.VMEM((chips * share * FLAT, 128), jnp.float32),
            pltpu.VMEM((chips * share, BS, 128), jnp.bfloat16),
            acc,
            acc,
            pltpu.VMEM((slot_count * FLAT, 128), jnp.float32),
            pltpu.SemaphoreType.DMA((3,)),
        ],
        compiler_params=pltpu.CompilerParams(vmem_limit_bytes=VMEM_LIMIT),
        cost_estimate=pl.CostEstimate(flops=flops, bytes_accessed=8 * 1024 * 1024, transcendentals=0),
        name="multiply",
    )(core, own_tasks, twin_tasks, panel, parts)


def exchange(x, axis):
    return lax.all_to_all(x, axis, split_axis=0, concat_axis=0, tiled=True)


def local(left_blocks, right_blocks, task_right, task_slot, recv_owner):
    columns, chips = lax.axis_size("x"), lax.axis_size("y")
    layers = lax.axis_size("z")
    group = ("y", "core")
    members = 2 * chips
    slot_count = recv_owner.shape[1]
    core = lax.axis_index("core").astype(jnp.int32).reshape(1)

    panel = exchange(repeat(left_blocks[0], chips), "y")
    rights = right_blocks[0, 0]
    tasks = jnp.concatenate([task_right[0], task_slot[0]], axis=0)
    twin_tasks = lax.ppermute(tasks, "core", SWAP)
    parts = pltpu.with_memory_space_constraint(prepare(rights, lax.ppermute(rights, "core", SWAP)), pltpu.HBM)
    mine, other = products(core, tasks, twin_tasks, panel, parts, slot_count, columns)
    mine = mine + lax.ppermute(other, "core", SWAP)
    run, width = mine.shape[2:]
    pieces = exchange(mine.reshape(columns * chips, run, width), ("x", "y"))
    piece = pieces.reshape(columns, chips, run, width).sum(axis=1).reshape(columns, layers, CAPACITY, width)
    piece = piece.transpose(1, 0, 2, 3).reshape(layers, columns * CAPACITY, width)
    received = exchange(piece, "z").reshape(slot_count, width)
    owners = recv_owner[0]
    owned_ids = jnp.arange(OWN_DEV * members, dtype=jnp.int32)
    selector = (owners[None, :] == owned_ids[:, None]).astype(jnp.float32)
    owned = jnp.dot(selector, received, precision=lax.Precision.HIGHEST, preferred_element_type=jnp.float32)
    own_blocks = exchange(owned.reshape(members, OWN_DEV, width), group)
    own_blocks = own_blocks.reshape(chips, 2, OWN_DEV, width).transpose(2, 1, 0, 3)
    return own_blocks.reshape(1, OWN_DEV, BLK)


def solution(mesh):
    rows, reps = mesh.shape["row"], mesh.shape["rep"]
    fine = Mesh(mesh.devices.reshape(rows // COLUMNS, COLUMNS, reps // 2, 2), ("z", "x", "y", "core"))
    row = ("z", "x")
    group = ("y", "core")
    in_specs = (
        P(row, group, None),
        P(row, group, None, None),
        P(row, group, None),
        P(row, group, None),
        P(row, None),
    )
    out_specs = P(row, group, None)
    return jax.shard_map(local, mesh=fine, in_specs=in_specs, out_specs=out_specs, check_vma=False)
```

```python
import jax
import jax.numpy as jnp
from jax import lax
from jax.experimental import pallas as pl
from jax.experimental.pallas import tpu as pltpu
from jax.sharding import Mesh
from jax.sharding import PartitionSpec as P

BS = 64
BLK = BS * BS
OWN_DEV = 2
CAPACITY = 2
COLUMNS = 4
VMEM_LIMIT = 24 * 1024 * 1024
ROWS = BLK // 128
FLAT = ROWS + 8
SWAP = [(0, 1), (1, 0)]


def low_half(shape):
    return lax.broadcasted_iota(jnp.int32, shape, len(shape) - 1) < BS


def split_rights(own_ref, twin_ref, parts_ref, spread_ref):
    count = own_ref.shape[0]
    mask = low_half((8, 128))

    for side, right_ref in enumerate((own_ref, twin_ref)):

        def unfold(group, carry, right_ref=right_ref, side=side):
            base = pl.multiple_of(group * 8, 8)
            spot = (side * count + base) * BS
            for m in range(ROWS):
                x = right_ref[pl.ds(base, 8), m * 128 : (m + 1) * 128]
                turned = pltpu.roll(x, BS, 1)
                spread_ref[pl.ds(spot + 2 * m, 8, stride=BS), :] = jnp.where(mask, x, turned)
                spread_ref[pl.ds(spot + 2 * m + 1, 8, stride=BS), :] = jnp.where(mask, turned, x)
            return carry

        lax.fori_loop(0, count // 8, unfold, 0)

    def cut(block, carry):
        x = spread_ref[pl.ds(pl.multiple_of(block * BS, BS), BS), :]
        coarse = x.astype(jnp.bfloat16)
        parts_ref[block, :BS, :] = coarse
        parts_ref[block, BS:, :] = (x - coarse.astype(jnp.float32)).astype(jnp.bfloat16)
        return carry

    lax.fori_loop(0, 2 * count, cut, 0, unroll=4)


def prepare(own, twin):
    count = own.shape[0]
    return pl.pallas_call(
        split_rights,
        out_shape=jax.ShapeDtypeStruct((2 * count, 2 * BS, 128), jnp.bfloat16),
        in_specs=[pl.BlockSpec(memory_space=pltpu.VMEM)] * 2,
        out_specs=pl.BlockSpec(memory_space=pltpu.VMEM),
        scratch_shapes=[pltpu.VMEM((2 * count * BS, 128), jnp.float32)],
        compiler_params=pltpu.CompilerParams(vmem_limit_bytes=VMEM_LIMIT),
        cost_estimate=pl.CostEstimate(flops=16 * count * BLK, bytes_accessed=24 * count * BLK, transcendentals=0),
        name="split_rights",
    )(own, twin)


def copy_out(x_ref, out_hbm, sems):
    copies = [pltpu.make_async_copy(x_ref, out_hbm.at[i], sems.at[i]) for i in range(out_hbm.shape[0])]
    for copy in copies:
        copy.start()
    for copy in copies:
        copy.wait()


def repeat(x, count):
    return pl.pallas_call(
        copy_out,
        out_shape=jax.ShapeDtypeStruct((count,) + x.shape, x.dtype),
        in_specs=[pl.BlockSpec(memory_space=pltpu.VMEM)],
        out_specs=pl.BlockSpec(memory_space=pltpu.HBM),
        scratch_shapes=[pltpu.SemaphoreType.DMA((count,))],
        name="repeat",
    )(x)


def multiply(
    core_ref, own_tasks_hbm, twin_tasks_hbm, left_ref, parts_hbm, mine_ref, other_ref,
    own_tasks_ref, twin_tasks_ref, parts_ref, flat_ref, lhs_ref, acc0, acc1, nat_ref, sems,
):
    copies = [
        pltpu.make_async_copy(source, target, sems.at[i])
        for i, (source, target) in enumerate(
            ((own_tasks_hbm, own_tasks_ref), (twin_tasks_hbm, twin_tasks_ref), (parts_hbm, parts_ref))
        )
    ]
    for copy in copies:
        copy.start()
    chips, share = left_ref.shape[0], left_ref.shape[1]
    count = chips * share
    per_block = own_tasks_ref.shape[1] // (2 * count)
    slot_count = acc0.shape[0]
    rights = parts_ref.shape[0] // 2
    core = core_ref[0]

    def clear(s, carry):
        acc0[s] = jnp.zeros(acc0.shape[1:], jnp.float32)
        acc1[s] = jnp.zeros(acc1.shape[1:], jnp.float32)
        return carry

    lax.fori_loop(0, slot_count, clear, 0, unroll=8)

    def unfold(chip, carry):
        for m in range(ROWS):
            flat_ref[pl.ds(chip * share * FLAT + m, share, stride=FLAT), :] = left_ref[chip, :, m * 128 : (m + 1) * 128]
        return carry

    lax.fori_loop(0, chips, unfold, 0)
    mask = low_half((ROWS, 128))
    wide = low_half((2 * BS, 128))

    def cut(k, carry):
        x = flat_ref[pl.ds(pl.multiple_of(k * FLAT, 8), ROWS), :]
        coarse = x.astype(jnp.bfloat16).astype(jnp.float32)
        fine = x - coarse
        lhs_ref[k, :ROWS, :] = jnp.where(mask, coarse, pltpu.roll(fine, BS, 1)).astype(jnp.bfloat16)
        lhs_ref[k, ROWS:, :] = jnp.where(mask, pltpu.roll(coarse, BS, 1), fine).astype(jnp.bfloat16)
        return carry

    lax.fori_loop(0, count, cut, 0, unroll=8)
    for copy in copies:
        copy.wait()

    def one_block(k, carry):
        tall = lhs_ref[k]
        lhs = jnp.concatenate([tall, tall], axis=1)
        first = ((k // share) * 2 * share + core * share + k % share) * per_block
        for side, tasks_ref in enumerate((own_tasks_ref, twin_tasks_ref)):
            for quad in range(per_block // 4):
                pairs = []
                for pair in range(2):
                    t = first + quad * 4 + pair * 2
                    low = parts_ref[side * rights + tasks_ref[0, t]]
                    high = parts_ref[side * rights + tasks_ref[0, t + 1]]
                    pairs.append(jnp.where(wide, low, high))
                both = jnp.concatenate(pairs, axis=1)
                rhs = jnp.concatenate([both[:BS], both[:BS], both[BS:], both[BS:]], axis=0)
                out = jnp.dot(lhs, rhs, preferred_element_type=jnp.float32)
                for pair in range(2):
                    t = first + quad * 4 + pair * 2
                    part = out[:, pair * 128 : (pair + 1) * 128]
                    acc0[tasks_ref[1, t]] += part
                    acc1[tasks_ref[1, t + 1]] += part
        return carry

    lax.fori_loop(0, count, one_block, 0, unroll=16)

    _, columns, run = mine_ref.shape[:3]
    capacity = CAPACITY

    def fold(s, carry):
        owner = s // capacity
        spot = (owner % columns) * run + (owner // columns) * capacity + s % capacity
        low, high = acc0[s], acc1[s]
        even = low[:ROWS] + pltpu.roll(high[:ROWS], BS, 1)
        odd = pltpu.roll(low[ROWS:], BS, 1) + high[ROWS:]
        nat_ref[pl.ds(pl.multiple_of(spot * FLAT, 8), ROWS), :] = jnp.where(mask, even, odd)
        return carry

    lax.fori_loop(0, slot_count, fold, 0, unroll=16)

    tiles = ROWS // (2 * chips)

    def place(column, carry):
        for group in range(run // 8):
            for out_ref, half in ((mine_ref, core), (other_ref, 1 - core)):
                first = (column * run + group * 8) * FLAT + half * (ROWS // 2)
                for m in range(ROWS // 2):
                    out_ref[m // tiles, column, group * 8 : (group + 1) * 8, (m % tiles) * 128 : (m % tiles + 1) * 128] = (
                        nat_ref[pl.ds(first + m, 8, stride=FLAT), :]
                    )
        return carry

    lax.fori_loop(0, columns, place, 0)


def products(core, own_tasks, twin_tasks, panel, parts, slot_count, columns):
    chips, share, _ = panel.shape
    smem = pl.BlockSpec(memory_space=pltpu.SMEM)
    vmem = pl.BlockSpec(memory_space=pltpu.VMEM)
    anywhere = pl.BlockSpec(memory_space=pl.ANY)
    acc = pltpu.VMEM((slot_count, BS, 128), jnp.float32)
    out = jax.ShapeDtypeStruct((chips, columns, slot_count // columns, BLK // (2 * chips)), jnp.float32)
    flops = 2 * own_tasks.shape[1] * BS * BS * BS * 4
    return pl.pallas_call(
        multiply,
        out_shape=(out, out),
        in_specs=[smem, anywhere, anywhere, vmem, pl.BlockSpec(memory_space=pltpu.HBM)],
        out_specs=(vmem, vmem),
        scratch_shapes=[
            pltpu.SMEM(own_tasks.shape, jnp.int32),
            pltpu.SMEM(twin_tasks.shape, jnp.int32),
            pltpu.VMEM(parts.shape, parts.dtype),
            pltpu.VMEM((chips * share * FLAT, 128), jnp.float32),
            pltpu.VMEM((chips * share, BS, 128), jnp.bfloat16),
            acc,
            acc,
            pltpu.VMEM((slot_count * FLAT, 128), jnp.float32),
            pltpu.SemaphoreType.DMA((3,)),
        ],
        compiler_params=pltpu.CompilerParams(vmem_limit_bytes=VMEM_LIMIT),
        cost_estimate=pl.CostEstimate(flops=flops, bytes_accessed=8 * 1024 * 1024, transcendentals=0),
        name="multiply",
    )(core, own_tasks, twin_tasks, panel, parts)


def exchange(x, axis):
    return lax.all_to_all(x, axis, split_axis=0, concat_axis=0, tiled=True)


def local(left_blocks, right_blocks, task_right, task_slot, recv_owner):
    columns, chips = lax.axis_size("x"), lax.axis_size("y")
    layers = lax.axis_size("z")
    group = ("y", "core")
    members = 2 * chips
    slot_count = recv_owner.shape[1]
    core = lax.axis_index("core").astype(jnp.int32).reshape(1)

    panel = exchange(repeat(left_blocks[0], chips), "y")
    rights = right_blocks[0, 0]
    tasks = jnp.concatenate([task_right[0], task_slot[0]], axis=0)
    twin_tasks = lax.ppermute(tasks, "core", SWAP)
    owned_ids = jnp.arange(OWN_DEV * members, dtype=jnp.int32).reshape(chips, 2, OWN_DEV).transpose(1, 0, 2).reshape(-1)
    selector = (recv_owner[0][None, :] == owned_ids[:, None]).astype(jnp.float32)
    parts = prepare(rights, lax.ppermute(rights, "core", SWAP))
    parts, selector = lax.optimization_barrier((parts, selector))
    parts = pltpu.with_memory_space_constraint(parts, pltpu.HBM)
    mine, other = products(core, tasks, twin_tasks, panel, parts, slot_count, columns)
    mine = mine + lax.ppermute(other, "core", SWAP)
    run, width = mine.shape[2:]
    pieces = exchange(mine.reshape(chips * columns, run, width), ("y", "x"))
    piece = pieces.reshape(chips, columns, run, width).sum(axis=0).reshape(columns, layers, CAPACITY, width)
    piece = piece.transpose(1, 0, 2, 3).reshape(layers, columns * CAPACITY, width)
    received = exchange(piece, "z").reshape(slot_count, width)
    owned = jnp.dot(selector, received, precision=lax.Precision.HIGHEST, preferred_element_type=jnp.float32)
    own_blocks = exchange(owned.reshape(members, OWN_DEV, width), ("core", "y"))
    return own_blocks.transpose(1, 0, 2).reshape(1, OWN_DEV, BLK)


def solution(mesh):
    rows, reps = mesh.shape["row"], mesh.shape["rep"]
    fine = Mesh(mesh.devices.reshape(rows // COLUMNS, COLUMNS, reps // 2, 2), ("z", "x", "y", "core"))
    row = ("z", "x")
    group = ("y", "core")
    in_specs = (
        P(row, group, None),
        P(row, group, None, None),
        P(row, group, None),
        P(row, group, None),
        P(row, None),
    )
    out_specs = P(row, group, None)
    return jax.shard_map(local, mesh=fine, in_specs=in_specs, out_specs=out_specs, check_vma=False)
```

```python
import jax
import jax.numpy as jnp
from jax import lax
from jax.experimental import pallas as pl
from jax.experimental.pallas import tpu as pltpu
from jax.sharding import Mesh
from jax.sharding import PartitionSpec as P

BS = 64
BLK = BS * BS
OWN_DEV = 2
CAPACITY = 2
COLUMNS = 4
VMEM_LIMIT = 24 * 1024 * 1024
ROWS = BLK // 128
FLAT = ROWS + 8
SWAP = [(0, 1), (1, 0)]


def low_half(shape):
    return lax.broadcasted_iota(jnp.int32, shape, len(shape) - 1) < BS


def split_rights(own_ref, twin_ref, parts_ref, spread_ref):
    count = own_ref.shape[0]
    mask = low_half((8, 128))

    for side, right_ref in enumerate((own_ref, twin_ref)):

        def unfold(group, carry, right_ref=right_ref, side=side):
            base = pl.multiple_of(group * 8, 8)
            spot = (side * count + base) * BS
            for m in range(ROWS):
                x = right_ref[pl.ds(base, 8), m * 128 : (m + 1) * 128]
                turned = pltpu.roll(x, BS, 1)
                spread_ref[pl.ds(spot + 2 * m, 8, stride=BS), :] = jnp.where(mask, x, turned)
                spread_ref[pl.ds(spot + 2 * m + 1, 8, stride=BS), :] = jnp.where(mask, turned, x)
            return carry

        lax.fori_loop(0, count // 8, unfold, 0)

    def cut(block, carry):
        x = spread_ref[pl.ds(pl.multiple_of(block * BS, BS), BS), :]
        coarse = x.astype(jnp.bfloat16)
        parts_ref[block, :BS, :] = coarse
        parts_ref[block, BS:, :] = (x - coarse.astype(jnp.float32)).astype(jnp.bfloat16)
        return carry

    lax.fori_loop(0, 2 * count, cut, 0, unroll=4)


def prepare(own, twin):
    count = own.shape[0]
    return pl.pallas_call(
        split_rights,
        out_shape=jax.ShapeDtypeStruct((2 * count, 2 * BS, 128), jnp.bfloat16),
        in_specs=[pl.BlockSpec(memory_space=pltpu.VMEM)] * 2,
        out_specs=pl.BlockSpec(memory_space=pltpu.VMEM),
        scratch_shapes=[pltpu.VMEM((2 * count * BS, 128), jnp.float32)],
        compiler_params=pltpu.CompilerParams(vmem_limit_bytes=VMEM_LIMIT),
        cost_estimate=pl.CostEstimate(flops=16 * count * BLK, bytes_accessed=24 * count * BLK, transcendentals=0),
        name="split_rights",
    )(own, twin)


def copy_out(x_ref, out_hbm, sems):
    copies = [pltpu.make_async_copy(x_ref, out_hbm.at[i], sems.at[i]) for i in range(out_hbm.shape[0])]
    for copy in copies:
        copy.start()
    for copy in copies:
        copy.wait()


def repeat(x, count):
    return pl.pallas_call(
        copy_out,
        out_shape=jax.ShapeDtypeStruct((count,) + x.shape, x.dtype),
        in_specs=[pl.BlockSpec(memory_space=pltpu.VMEM)],
        out_specs=pl.BlockSpec(memory_space=pltpu.HBM),
        scratch_shapes=[pltpu.SemaphoreType.DMA((count,))],
        name="repeat",
    )(x)


def multiply(
    core_ref, own_tasks_hbm, twin_tasks_hbm, left_ref, parts_hbm, mine_ref, other_ref,
    own_tasks_ref, twin_tasks_ref, parts_ref, flat_ref, lhs_ref, acc0, acc1, nat_ref, sems,
):
    copies = [
        pltpu.make_async_copy(source, target, sems.at[i])
        for i, (source, target) in enumerate(
            ((own_tasks_hbm, own_tasks_ref), (twin_tasks_hbm, twin_tasks_ref), (parts_hbm, parts_ref))
        )
    ]
    for copy in copies:
        copy.start()
    chips, share = left_ref.shape[0], left_ref.shape[1]
    count = chips * share
    per_block = own_tasks_ref.shape[1] // (2 * count)
    slot_count = acc0.shape[0]
    rights = parts_ref.shape[0] // 2
    core = core_ref[0]

    def clear(s, carry):
        acc0[s] = jnp.zeros(acc0.shape[1:], jnp.float32)
        acc1[s] = jnp.zeros(acc1.shape[1:], jnp.float32)
        return carry

    lax.fori_loop(0, slot_count, clear, 0, unroll=8)

    def unfold(chip, carry):
        for m in range(ROWS):
            flat_ref[pl.ds(chip * share * FLAT + m, share, stride=FLAT), :] = left_ref[chip, :, m * 128 : (m + 1) * 128]
        return carry

    lax.fori_loop(0, chips, unfold, 0)
    mask = low_half((ROWS, 128))
    wide = low_half((2 * BS, 128))

    def cut(k, carry):
        x = flat_ref[pl.ds(pl.multiple_of(k * FLAT, 8), ROWS), :]
        coarse = x.astype(jnp.bfloat16).astype(jnp.float32)
        fine = x - coarse
        turned = pltpu.roll(jnp.where(mask, fine, coarse), BS, 1)
        lhs_ref[k, :ROWS, :] = jnp.where(mask, coarse, turned).astype(jnp.bfloat16)
        lhs_ref[k, ROWS:, :] = jnp.where(mask, turned, fine).astype(jnp.bfloat16)
        return carry

    lax.fori_loop(0, count, cut, 0, unroll=16)
    for copy in copies:
        copy.wait()

    def one_block(k, carry):
        tall = lhs_ref[k]
        lhs = jnp.concatenate([tall, tall], axis=1)
        first = ((k // share) * 2 * share + core * share + k % share) * per_block
        for side, tasks_ref in enumerate((own_tasks_ref, twin_tasks_ref)):
            for quad in range(per_block // 4):
                pairs = []
                for pair in range(2):
                    t = first + quad * 4 + pair * 2
                    low = parts_ref[side * rights + tasks_ref[0, t]]
                    high = parts_ref[side * rights + tasks_ref[0, t + 1]]
                    pairs.append(jnp.where(wide, low, high))
                both = jnp.concatenate(pairs, axis=1)
                rhs = jnp.concatenate([both[:BS], both[:BS], both[BS:], both[BS:]], axis=0)
                out = jnp.dot(lhs, rhs, preferred_element_type=jnp.float32)
                for pair in range(2):
                    t = first + quad * 4 + pair * 2
                    part = out[:, pair * 128 : (pair + 1) * 128]
                    acc0[tasks_ref[1, t]] += part
                    acc1[tasks_ref[1, t + 1]] += part
        return carry

    lax.fori_loop(0, count, one_block, 0, unroll=32)

    _, columns, run = mine_ref.shape[:3]
    capacity = CAPACITY

    def fold(s, carry):
        owner = s // capacity
        spot = (owner % columns) * run + (owner // columns) * capacity + s % capacity
        low, high = acc0[s], acc1[s]
        straight = jnp.where(mask, low[:ROWS], high[ROWS:])
        turned = pltpu.roll(jnp.where(mask, low[ROWS:], high[:ROWS]), BS, 1)
        nat_ref[pl.ds(pl.multiple_of(spot * FLAT, 8), ROWS), :] = straight + turned
        return carry

    lax.fori_loop(0, slot_count, fold, 0, unroll=32)

    tiles = ROWS // (2 * chips)

    def place(column, carry):
        for group in range(run // 8):
            for out_ref, half in ((mine_ref, core), (other_ref, 1 - core)):
                first = (column * run + group * 8) * FLAT + half * (ROWS // 2)
                for m in range(ROWS // 2):
                    out_ref[m // tiles, column, group * 8 : (group + 1) * 8, (m % tiles) * 128 : (m % tiles + 1) * 128] = (
                        nat_ref[pl.ds(first + m, 8, stride=FLAT), :]
                    )
        return carry

    lax.fori_loop(0, columns, place, 0)


def products(core, own_tasks, twin_tasks, panel, parts, slot_count, columns):
    chips, share, _ = panel.shape
    smem = pl.BlockSpec(memory_space=pltpu.SMEM)
    vmem = pl.BlockSpec(memory_space=pltpu.VMEM)
    anywhere = pl.BlockSpec(memory_space=pl.ANY)
    acc = pltpu.VMEM((slot_count, BS, 128), jnp.float32)
    out = jax.ShapeDtypeStruct((chips, columns, slot_count // columns, BLK // (2 * chips)), jnp.float32)
    flops = 2 * own_tasks.shape[1] * BS * BS * BS * 4
    return pl.pallas_call(
        multiply,
        out_shape=(out, out),
        in_specs=[smem, anywhere, anywhere, vmem, pl.BlockSpec(memory_space=pltpu.HBM)],
        out_specs=(vmem, vmem),
        scratch_shapes=[
            pltpu.SMEM(own_tasks.shape, jnp.int32),
            pltpu.SMEM(twin_tasks.shape, jnp.int32),
            pltpu.VMEM(parts.shape, parts.dtype),
            pltpu.VMEM((chips * share * FLAT, 128), jnp.float32),
            pltpu.VMEM((chips * share, BS, 128), jnp.bfloat16),
            acc,
            acc,
            pltpu.VMEM((slot_count * FLAT, 128), jnp.float32),
            pltpu.SemaphoreType.DMA((3,)),
        ],
        compiler_params=pltpu.CompilerParams(vmem_limit_bytes=VMEM_LIMIT),
        cost_estimate=pl.CostEstimate(flops=flops, bytes_accessed=8 * 1024 * 1024, transcendentals=0),
        name="multiply",
    )(core, own_tasks, twin_tasks, panel, parts)


def exchange(x, axis):
    return lax.all_to_all(x, axis, split_axis=0, concat_axis=0, tiled=True)


def local(left_blocks, right_blocks, task_right, task_slot, recv_owner):
    columns, chips = lax.axis_size("x"), lax.axis_size("y")
    layers = lax.axis_size("z")
    group = ("y", "core")
    members = 2 * chips
    slot_count = recv_owner.shape[1]
    core = lax.axis_index("core").astype(jnp.int32).reshape(1)

    panel = exchange(repeat(left_blocks[0], chips), "y")
    rights = right_blocks[0, 0]
    tasks = jnp.concatenate([task_right[0], task_slot[0]], axis=0)
    twin_tasks = lax.ppermute(tasks, "core", SWAP)
    owned_ids = jnp.arange(OWN_DEV * members, dtype=jnp.int32).reshape(chips, 2, OWN_DEV).transpose(1, 0, 2).reshape(-1)
    selector = (recv_owner[0][None, :] == owned_ids[:, None]).astype(jnp.float32)
    parts = prepare(rights, lax.ppermute(rights, "core", SWAP))
    parts, selector = lax.optimization_barrier((parts, selector))
    parts = pltpu.with_memory_space_constraint(parts, pltpu.HBM)
    mine, other = products(core, tasks, twin_tasks, panel, parts, slot_count, columns)
    mine = mine + lax.ppermute(other, "core", SWAP)
    run, width = mine.shape[2:]
    pieces = exchange(mine.reshape(chips * columns, run, width), ("y", "x"))
    piece = pieces.reshape(chips, columns, run, width).sum(axis=0).reshape(columns, layers, CAPACITY, width)
    piece = piece.transpose(1, 0, 2, 3).reshape(layers, columns * CAPACITY, width)
    received = exchange(piece, "z").reshape(slot_count, width)
    owned = jnp.dot(selector, received, precision=lax.Precision.HIGHEST, preferred_element_type=jnp.float32)
    own_blocks = exchange(owned.reshape(members, OWN_DEV, width), ("core", "y"))
    return own_blocks.transpose(1, 0, 2).reshape(1, OWN_DEV, BLK)


def solution(mesh):
    rows, reps = mesh.shape["row"], mesh.shape["rep"]
    fine = Mesh(mesh.devices.reshape(rows // COLUMNS, COLUMNS, reps // 2, 2), ("z", "x", "y", "core"))
    row = ("z", "x")
    group = ("y", "core")
    in_specs = (
        P(row, group, None),
        P(row, group, None, None),
        P(row, group, None),
        P(row, group, None),
        P(row, None),
    )
    out_specs = P(row, group, None)
    return jax.shard_map(local, mesh=fine, in_specs=in_specs, out_specs=out_specs, check_vma=False)
```

```python
import jax
import jax.numpy as jnp
from jax import lax
from jax.experimental import pallas as pl
from jax.experimental.pallas import tpu as pltpu
from jax.sharding import Mesh
from jax.sharding import PartitionSpec as P

BS = 64
BLK = BS * BS
OWN_DEV = 2
CAPACITY = 2
COLUMNS = 4
VMEM_LIMIT = 24 * 1024 * 1024
ROWS = BLK // 128
FLAT = ROWS + 8
SWAP = [(0, 1), (1, 0)]


def low_half(shape):
    return lax.broadcasted_iota(jnp.int32, shape, len(shape) - 1) < BS


def split_rights(own_ref, twin_ref, parts_ref, spread_ref):
    count = own_ref.shape[0]
    mask = low_half((8, 128))

    for side, right_ref in enumerate((own_ref, twin_ref)):

        def unfold(group, carry, right_ref=right_ref, side=side):
            base = pl.multiple_of(group * 8, 8)
            spot = (side * count + base) * BS
            for m in range(ROWS):
                x = right_ref[pl.ds(base, 8), m * 128 : (m + 1) * 128]
                turned = pltpu.roll(x, BS, 1)
                spread_ref[pl.ds(spot + 2 * m, 8, stride=BS), :] = jnp.where(mask, x, turned)
                spread_ref[pl.ds(spot + 2 * m + 1, 8, stride=BS), :] = jnp.where(mask, turned, x)
            return carry

        lax.fori_loop(0, count // 8, unfold, 0)

    def cut(block, carry):
        x = spread_ref[pl.ds(pl.multiple_of(block * BS, BS), BS), :]
        coarse = x.astype(jnp.bfloat16)
        parts_ref[block, :BS, :] = coarse
        parts_ref[block, BS:, :] = (x - coarse.astype(jnp.float32)).astype(jnp.bfloat16)
        return carry

    lax.fori_loop(0, 2 * count, cut, 0, unroll=4)


def prepare(own, twin):
    count = own.shape[0]
    return pl.pallas_call(
        split_rights,
        out_shape=jax.ShapeDtypeStruct((2 * count, 2 * BS, 128), jnp.bfloat16),
        in_specs=[pl.BlockSpec(memory_space=pltpu.VMEM)] * 2,
        out_specs=pl.BlockSpec(memory_space=pltpu.VMEM),
        scratch_shapes=[pltpu.VMEM(((2 * count + 8) * BS, 128), jnp.float32)],
        compiler_params=pltpu.CompilerParams(vmem_limit_bytes=VMEM_LIMIT),
        cost_estimate=pl.CostEstimate(flops=16 * count * BLK, bytes_accessed=24 * count * BLK, transcendentals=0),
        name="split_rights",
    )(own, twin)


def copy_out(x_ref, out_hbm, sems):
    copies = [pltpu.make_async_copy(x_ref, out_hbm.at[i], sems.at[i]) for i in range(out_hbm.shape[0])]
    for copy in copies:
        copy.start()
    for copy in copies:
        copy.wait()


def repeat(x, count):
    return pl.pallas_call(
        copy_out,
        out_shape=jax.ShapeDtypeStruct((count,) + x.shape, x.dtype),
        in_specs=[pl.BlockSpec(memory_space=pltpu.VMEM)],
        out_specs=pl.BlockSpec(memory_space=pltpu.HBM),
        scratch_shapes=[pltpu.SemaphoreType.DMA((count,))],
        name="repeat",
    )(x)


def multiply(
    core_ref, own_tasks_hbm, twin_tasks_hbm, left_ref, parts_hbm, mine_ref, other_ref,
    own_tasks_ref, twin_tasks_ref, parts_ref, flat_ref, lhs_ref, acc0, acc1, nat_ref, sems,
):
    copies = [
        pltpu.make_async_copy(source, target, sems.at[i])
        for i, (source, target) in enumerate(
            ((own_tasks_hbm, own_tasks_ref), (twin_tasks_hbm, twin_tasks_ref), (parts_hbm, parts_ref))
        )
    ]
    for copy in copies:
        copy.start()
    chips, share = left_ref.shape[0], left_ref.shape[1]
    count = chips * share
    per_block = own_tasks_ref.shape[1] // (2 * count)
    slot_count = acc0.shape[0]
    rights = parts_ref.shape[0] // 2
    core = core_ref[0]

    def clear(s, carry):
        acc0[s] = jnp.zeros(acc0.shape[1:], jnp.float32)
        acc1[s] = jnp.zeros(acc1.shape[1:], jnp.float32)
        return carry

    lax.fori_loop(0, slot_count, clear, 0, unroll=8)

    def unfold(chip, carry):
        for m in range(ROWS):
            flat_ref[pl.ds(chip * share * FLAT + m, share, stride=FLAT), :] = left_ref[chip, :, m * 128 : (m + 1) * 128]
        return carry

    lax.fori_loop(0, chips, unfold, 0)
    mask = low_half((ROWS, 128))
    wide = low_half((2 * BS, 128))

    def cut(k, carry):
        x = flat_ref[pl.ds(pl.multiple_of(k * FLAT, 8), ROWS), :]
        coarse = x.astype(jnp.bfloat16).astype(jnp.float32)
        fine = x - coarse
        turned = pltpu.roll(jnp.where(mask, fine, coarse), BS, 1)
        lhs_ref[k, :ROWS, :] = jnp.where(mask, coarse, turned).astype(jnp.bfloat16)
        lhs_ref[k, ROWS:, :] = jnp.where(mask, turned, fine).astype(jnp.bfloat16)
        return carry

    lax.fori_loop(0, count, cut, 0, unroll=16)
    for copy in copies:
        copy.wait()

    def one_block(k, carry):
        tall = lhs_ref[k]
        lhs = jnp.concatenate([tall, tall], axis=1)
        first = ((k // share) * 2 * share + core * share + k % share) * per_block
        for side, tasks_ref in enumerate((own_tasks_ref, twin_tasks_ref)):
            for quad in range(per_block // 4):
                pairs = []
                for pair in range(2):
                    t = first + quad * 4 + pair * 2
                    low = parts_ref[side * rights + tasks_ref[0, t]]
                    high = parts_ref[side * rights + tasks_ref[0, t + 1]]
                    pairs.append(jnp.where(wide, low, high))
                both = jnp.concatenate(pairs, axis=1)
                rhs = jnp.concatenate([both[:BS], both[:BS], both[BS:], both[BS:]], axis=0)
                out = jnp.dot(lhs, rhs, preferred_element_type=jnp.float32)
                for pair in range(2):
                    t = first + quad * 4 + pair * 2
                    part = out[:, pair * 128 : (pair + 1) * 128]
                    acc0[tasks_ref[1, t]] += part
                    acc1[tasks_ref[1, t + 1]] += part
        return carry

    lax.fori_loop(0, count, one_block, 0, unroll=32)

    _, columns, run = mine_ref.shape[:3]
    capacity = CAPACITY

    def fold(s, carry):
        owner = s // capacity
        spot = (owner % columns) * run + (owner // columns) * capacity + s % capacity
        low, high = acc0[s], acc1[s]
        straight = jnp.where(mask, low[:ROWS], high[ROWS:])
        turned = pltpu.roll(jnp.where(mask, low[ROWS:], high[:ROWS]), BS, 1)
        nat_ref[pl.ds(pl.multiple_of(spot * FLAT, 8), ROWS), :] = straight + turned
        return carry

    lax.fori_loop(0, slot_count, fold, 0, unroll=32)

    tiles = ROWS // (2 * chips)

    def place(column, carry):
        for group in range(run // 8):
            for out_ref, half in ((mine_ref, core), (other_ref, 1 - core)):
                first = (column * run + group * 8) * FLAT + half * (ROWS // 2)
                for m in range(ROWS // 2):
                    out_ref[m // tiles, column, group * 8 : (group + 1) * 8, (m % tiles) * 128 : (m % tiles + 1) * 128] = (
                        nat_ref[pl.ds(first + m, 8, stride=FLAT), :]
                    )
        return carry

    lax.fori_loop(0, columns, place, 0)


def products(core, own_tasks, twin_tasks, panel, parts, slot_count, columns):
    chips, share, _ = panel.shape
    smem = pl.BlockSpec(memory_space=pltpu.SMEM)
    vmem = pl.BlockSpec(memory_space=pltpu.VMEM)
    anywhere = pl.BlockSpec(memory_space=pl.ANY)
    acc = pltpu.VMEM((slot_count, BS, 128), jnp.float32)
    out = jax.ShapeDtypeStruct((chips, columns, slot_count // columns, BLK // (2 * chips)), jnp.float32)
    flops = 2 * own_tasks.shape[1] * BS * BS * BS * 4
    return pl.pallas_call(
        multiply,
        out_shape=(out, out),
        in_specs=[smem, anywhere, anywhere, vmem, pl.BlockSpec(memory_space=pltpu.HBM)],
        out_specs=(vmem, vmem),
        scratch_shapes=[
            pltpu.SMEM(own_tasks.shape, jnp.int32),
            pltpu.SMEM(twin_tasks.shape, jnp.int32),
            pltpu.VMEM(parts.shape, parts.dtype),
            pltpu.VMEM(((chips * share + 8) * FLAT, 128), jnp.float32),
            pltpu.VMEM((chips * share, BS, 128), jnp.bfloat16),
            acc,
            acc,
            pltpu.VMEM(((slot_count + 8) * FLAT, 128), jnp.float32),
            pltpu.SemaphoreType.DMA((3,)),
        ],
        compiler_params=pltpu.CompilerParams(vmem_limit_bytes=VMEM_LIMIT),
        cost_estimate=pl.CostEstimate(flops=flops, bytes_accessed=8 * 1024 * 1024, transcendentals=0),
        name="multiply",
    )(core, own_tasks, twin_tasks, panel, parts)


def exchange(x, axis):
    return lax.all_to_all(x, axis, split_axis=0, concat_axis=0, tiled=True)


def local(left_blocks, right_blocks, task_right, task_slot, recv_owner):
    columns, chips = lax.axis_size("x"), lax.axis_size("y")
    layers = lax.axis_size("z")
    group = ("y", "core")
    members = 2 * chips
    slot_count = recv_owner.shape[1]
    core = lax.axis_index("core").astype(jnp.int32).reshape(1)

    panel = exchange(repeat(left_blocks[0], chips), "y")
    rights = right_blocks[0, 0]
    tasks = jnp.concatenate([task_right[0], task_slot[0]], axis=0)
    twin_tasks = lax.ppermute(tasks, "core", SWAP)
    owned_ids = jnp.arange(OWN_DEV * members, dtype=jnp.int32).reshape(chips, 2, OWN_DEV).transpose(1, 0, 2).reshape(-1)
    selector = (recv_owner[0][None, :] == owned_ids[:, None]).astype(jnp.float32)
    parts = prepare(rights, lax.ppermute(rights, "core", SWAP))
    parts, selector = lax.optimization_barrier((parts, selector))
    parts = pltpu.with_memory_space_constraint(parts, pltpu.HBM)
    mine, other = products(core, tasks, twin_tasks, panel, parts, slot_count, columns)
    mine = mine + lax.ppermute(other, "core", SWAP)
    run, width = mine.shape[2:]
    pieces = exchange(mine.reshape(chips * columns, run, width), ("y", "x"))
    piece = pieces.reshape(chips, columns, run, width).sum(axis=0).reshape(columns, layers, CAPACITY, width)
    piece = piece.transpose(1, 0, 2, 3).reshape(layers, columns * CAPACITY, width)
    received = exchange(piece, "z").reshape(slot_count, width)
    owned = jnp.dot(selector, received, precision=lax.Precision.HIGHEST, preferred_element_type=jnp.float32)
    own_blocks = exchange(owned.reshape(members, OWN_DEV, width), ("core", "y"))
    return own_blocks.transpose(1, 0, 2).reshape(1, OWN_DEV, BLK)


def solution(mesh):
    rows, reps = mesh.shape["row"], mesh.shape["rep"]
    fine = Mesh(mesh.devices.reshape(rows // COLUMNS, COLUMNS, reps // 2, 2), ("z", "x", "y", "core"))
    row = ("z", "x")
    group = ("y", "core")
    in_specs = (
        P(row, group, None),
        P(row, group, None, None),
        P(row, group, None),
        P(row, group, None),
        P(row, None),
    )
    out_specs = P(row, group, None)
    return jax.shard_map(local, mesh=fine, in_specs=in_specs, out_specs=out_specs, check_vma=False)
```

```python
import jax
import jax.numpy as jnp
from jax import lax
from jax.experimental import pallas as pl
from jax.experimental.pallas import tpu as pltpu
from jax.sharding import Mesh
from jax.sharding import PartitionSpec as P

BS = 64
BLK = BS * BS
OWN_DEV = 2
CAPACITY = 2
COLUMNS = 4
VMEM_LIMIT = 24 * 1024 * 1024
ROWS = BLK // 128
FLAT = ROWS + 8
SWAP = [(0, 1), (1, 0)]


def low_half(shape):
    return lax.broadcasted_iota(jnp.int32, shape, len(shape) - 1) < BS


def split_rights(own_ref, twin_ref, parts_ref, spread_ref):
    count = own_ref.shape[0]
    mask = low_half((8, 128))

    for side, right_ref in enumerate((own_ref, twin_ref)):

        def unfold(group, carry, right_ref=right_ref, side=side):
            base = pl.multiple_of(group * 8, 8)
            spot = (side * count + base) * BS
            for m in range(ROWS):
                x = right_ref[pl.ds(base, 8), m * 128 : (m + 1) * 128]
                turned = pltpu.roll(x, BS, 1)
                spread_ref[pl.ds(spot + 2 * m, 8, stride=BS), :] = jnp.where(mask, x, turned)
                spread_ref[pl.ds(spot + 2 * m + 1, 8, stride=BS), :] = jnp.where(mask, turned, x)
            return carry

        lax.fori_loop(0, count // 8, unfold, 0)

    def cut(block, carry):
        x = spread_ref[pl.ds(pl.multiple_of(block * BS, BS), BS), :]
        coarse = x.astype(jnp.bfloat16)
        parts_ref[block, :BS, :] = coarse
        parts_ref[block, BS:, :] = (x - coarse.astype(jnp.float32)).astype(jnp.bfloat16)
        return carry

    lax.fori_loop(0, 2 * count, cut, 0, unroll=4)


def prepare(own, twin):
    count = own.shape[0]
    return pl.pallas_call(
        split_rights,
        out_shape=jax.ShapeDtypeStruct((2 * count, 2 * BS, 128), jnp.bfloat16),
        in_specs=[pl.BlockSpec(memory_space=pltpu.VMEM)] * 2,
        out_specs=pl.BlockSpec(memory_space=pltpu.VMEM),
        scratch_shapes=[pltpu.VMEM(((2 * count + 8) * BS, 128), jnp.float32)],
        compiler_params=pltpu.CompilerParams(vmem_limit_bytes=VMEM_LIMIT),
        cost_estimate=pl.CostEstimate(flops=16 * count * BLK, bytes_accessed=24 * count * BLK, transcendentals=0),
        name="split_rights",
    )(own, twin)


def copy_out(x_ref, out_hbm, sems):
    copies = [pltpu.make_async_copy(x_ref, out_hbm.at[i], sems.at[i]) for i in range(out_hbm.shape[0])]
    for copy in copies:
        copy.start()
    for copy in copies:
        copy.wait()


def repeat(x, count):
    return pl.pallas_call(
        copy_out,
        out_shape=jax.ShapeDtypeStruct((count,) + x.shape, x.dtype),
        in_specs=[pl.BlockSpec(memory_space=pltpu.VMEM)],
        out_specs=pl.BlockSpec(memory_space=pltpu.HBM),
        scratch_shapes=[pltpu.SemaphoreType.DMA((count,))],
        name="repeat",
    )(x)


def multiply(
    core_ref, own_tasks_hbm, twin_tasks_hbm, left_ref, parts_hbm, mine_ref, other_ref,
    own_tasks_ref, twin_tasks_ref, parts_ref, flat_ref, lhs_ref, acc0, acc1, nat_ref, sems,
):
    copies = [
        pltpu.make_async_copy(source, target, sems.at[i])
        for i, (source, target) in enumerate(
            ((own_tasks_hbm, own_tasks_ref), (twin_tasks_hbm, twin_tasks_ref), (parts_hbm, parts_ref))
        )
    ]
    for copy in copies:
        copy.start()
    chips, share = left_ref.shape[0], left_ref.shape[1]
    count = chips * share
    per_block = own_tasks_ref.shape[1] // (2 * count)
    slot_count = acc0.shape[0]
    rights = parts_ref.shape[0] // 2
    core = core_ref[0]

    def clear(s, carry):
        acc0[s] = jnp.zeros(acc0.shape[1:], jnp.float32)
        acc1[s] = jnp.zeros(acc1.shape[1:], jnp.float32)
        return carry

    lax.fori_loop(0, slot_count, clear, 0, unroll=8)

    def unfold(chip, carry):
        for m in range(ROWS):
            flat_ref[pl.ds(chip * share * FLAT + m, share, stride=FLAT), :] = left_ref[chip, :, m * 128 : (m + 1) * 128]
        return carry

    lax.fori_loop(0, chips, unfold, 0)
    mask = low_half((ROWS, 128))
    wide = low_half((2 * BS, 128))

    def cut(k, carry):
        x = flat_ref[pl.ds(pl.multiple_of(k * FLAT, 8), ROWS), :]
        coarse = x.astype(jnp.bfloat16).astype(jnp.float32)
        fine = x - coarse
        turned = pltpu.roll(jnp.where(mask, fine, coarse), BS, 1)
        lhs_ref[k, :ROWS, :] = jnp.where(mask, coarse, turned).astype(jnp.bfloat16)
        lhs_ref[k, ROWS:, :] = jnp.where(mask, turned, fine).astype(jnp.bfloat16)
        return carry

    lax.fori_loop(0, count, cut, 0, unroll=16)
    for copy in copies:
        copy.wait()

    def one_block(k, carry):
        tall = lhs_ref[k]
        lhs = jnp.concatenate([tall, tall], axis=1)
        first = ((k // share) * 2 * share + core * share + k % share) * per_block
        for side, tasks_ref in enumerate((own_tasks_ref, twin_tasks_ref)):
            for quad in range(per_block // 4):
                pairs = []
                for pair in range(2):
                    t = first + quad * 4 + pair * 2
                    low = parts_ref[side * rights + tasks_ref[0, t]]
                    high = parts_ref[side * rights + tasks_ref[0, t + 1]]
                    pairs.append(jnp.where(wide, low, high))
                both = jnp.concatenate(pairs, axis=1)
                rhs = jnp.concatenate([both[:BS], both[:BS], both[BS:], both[BS:]], axis=0)
                out = jnp.dot(lhs, rhs, preferred_element_type=jnp.float32)
                for pair in range(2):
                    t = first + quad * 4 + pair * 2
                    part = out[:, pair * 128 : (pair + 1) * 128]
                    acc0[tasks_ref[1, t]] += part
                    acc1[tasks_ref[1, t + 1]] += part
        return carry

    lax.fori_loop(0, count, one_block, 0, unroll=32)

    _, columns, run = mine_ref.shape[:3]
    capacity = CAPACITY

    def fold(s, carry):
        owner = s // capacity
        spot = (owner % columns) * run + (owner // columns) * capacity + s % capacity
        low, high = acc0[s], acc1[s]
        straight = jnp.where(mask, low[:ROWS], high[ROWS:])
        turned = pltpu.roll(jnp.where(mask, low[ROWS:], high[:ROWS]), BS, 1)
        nat_ref[pl.ds(pl.multiple_of(spot * FLAT, 8), ROWS), :] = straight + turned
        return carry

    lax.fori_loop(0, slot_count, fold, 0, unroll=16)

    tiles = ROWS // (2 * chips)

    def place(column, carry):
        for group in range(run // 8):
            for out_ref, half in ((mine_ref, core), (other_ref, 1 - core)):
                first = (column * run + group * 8) * FLAT + half * (ROWS // 2)
                for m in range(ROWS // 2):
                    out_ref[m // tiles, column, group * 8 : (group + 1) * 8, (m % tiles) * 128 : (m % tiles + 1) * 128] = (
                        nat_ref[pl.ds(first + m, 8, stride=FLAT), :]
                    )
        return carry

    lax.fori_loop(0, columns, place, 0)


def products(core, own_tasks, twin_tasks, panel, parts, slot_count, columns):
    chips, share, _ = panel.shape
    smem = pl.BlockSpec(memory_space=pltpu.SMEM)
    vmem = pl.BlockSpec(memory_space=pltpu.VMEM)
    anywhere = pl.BlockSpec(memory_space=pl.ANY)
    acc = pltpu.VMEM((slot_count, BS, 128), jnp.float32)
    out = jax.ShapeDtypeStruct((chips, columns, slot_count // columns, BLK // (2 * chips)), jnp.float32)
    flops = 2 * own_tasks.shape[1] * BS * BS * BS * 4
    return pl.pallas_call(
        multiply,
        out_shape=(out, out),
        in_specs=[smem, anywhere, anywhere, vmem, pl.BlockSpec(memory_space=pltpu.HBM)],
        out_specs=(vmem, vmem),
        scratch_shapes=[
            pltpu.SMEM(own_tasks.shape, jnp.int32),
            pltpu.SMEM(twin_tasks.shape, jnp.int32),
            pltpu.VMEM(parts.shape, parts.dtype),
            pltpu.VMEM(((chips * share + 8) * FLAT, 128), jnp.float32),
            pltpu.VMEM((chips * share, BS, 128), jnp.bfloat16),
            acc,
            acc,
            pltpu.VMEM(((slot_count + 8) * FLAT, 128), jnp.float32),
            pltpu.SemaphoreType.DMA((3,)),
        ],
        compiler_params=pltpu.CompilerParams(vmem_limit_bytes=VMEM_LIMIT),
        cost_estimate=pl.CostEstimate(flops=flops, bytes_accessed=8 * 1024 * 1024, transcendentals=0),
        name="multiply",
    )(core, own_tasks, twin_tasks, panel, parts)


def exchange(x, axis):
    return lax.all_to_all(x, axis, split_axis=0, concat_axis=0, tiled=True)


def local(left_blocks, right_blocks, task_right, task_slot, recv_owner):
    columns, chips = lax.axis_size("x"), lax.axis_size("y")
    layers = lax.axis_size("z")
    group = ("y", "core")
    members = 2 * chips
    slot_count = recv_owner.shape[1]
    core = lax.axis_index("core").astype(jnp.int32).reshape(1)

    panel = exchange(repeat(left_blocks[0], chips), "y")
    rights = right_blocks[0, 0]
    tasks = jnp.concatenate([task_right[0], task_slot[0]], axis=0)
    twin_tasks = lax.ppermute(tasks, "core", SWAP)
    owned_ids = jnp.arange(OWN_DEV * members, dtype=jnp.int32).reshape(chips, 2, OWN_DEV).transpose(1, 0, 2).reshape(-1)
    selector = (recv_owner[0][None, :] == owned_ids[:, None]).astype(jnp.float32)
    parts = prepare(rights, lax.ppermute(rights, "core", SWAP))
    parts, selector = lax.optimization_barrier((parts, selector))
    parts = pltpu.with_memory_space_constraint(parts, pltpu.HBM)
    mine, other = products(core, tasks, twin_tasks, panel, parts, slot_count, columns)
    mine = mine + lax.ppermute(other, "core", SWAP)
    run, width = mine.shape[2:]
    pieces = exchange(mine.reshape(chips * columns, run, width), ("y", "x"))
    piece = pieces.reshape(chips, columns, run, width).sum(axis=0).reshape(columns, layers, CAPACITY, width)
    piece = piece.transpose(1, 0, 2, 3).reshape(layers, columns * CAPACITY, width)
    received = exchange(piece, "z").reshape(slot_count, width)
    owned = jnp.dot(selector, received, precision=lax.Precision.HIGHEST, preferred_element_type=jnp.float32)
    own_blocks = exchange(owned.reshape(members, OWN_DEV, width), ("core", "y"))
    return own_blocks.transpose(1, 0, 2).reshape(1, OWN_DEV, BLK)


def solution(mesh):
    rows, reps = mesh.shape["row"], mesh.shape["rep"]
    fine = Mesh(mesh.devices.reshape(rows // COLUMNS, COLUMNS, reps // 2, 2), ("z", "x", "y", "core"))
    row = ("z", "x")
    group = ("y", "core")
    in_specs = (
        P(row, group, None),
        P(row, group, None, None),
        P(row, group, None),
        P(row, group, None),
        P(row, None),
    )
    out_specs = P(row, group, None)
    return jax.shard_map(local, mesh=fine, in_specs=in_specs, out_specs=out_specs, check_vma=False)
```
